32 devices in a mesh: parts: 2 (over y), wide: 8 (over z, x), tensor: 2 (over core).
Axes of the slice: x: 2, y: 2, z: 4, core: 2. Of those that a mesh axis runs over, the one named last changes fastest.
Arguments:
- tokens: bfloat16 [256, 8192], P(('parts', 'wide'), 'tensor'), parts along dimension 0, may hold values from -6 to 6
- gate_weight: bfloat16 [8192, 16384], P('tensor', 'wide'), may hold values from -0.0625 to 0.0625
- up_weight: bfloat16 [8192, 16384], P('tensor', 'wide'), may hold values from -0.0625 to 0.0625
- down_weight: bfloat16 [16384, 8192], P('wide', 'tensor'), may hold values from -0.046875 to 0.046875
- adapter_down: bfloat16 [128, 16, 16384], P('parts', None, 'wide'), parts along dimension 0, may hold values from -0.046875 to 0.046875
- adapter_up: bfloat16 [128, 16, 8192], P(('parts', 'wide'), None, 'tensor'), parts along dimension 0, may hold values from -1.5 to 1.5
- row_adapter: int32 [256], P('parts'), parts along dimension 0, may hold values from 0 to 63, as said below
- block_first: int32 [20], P('parts'), parts along dimension 0, may hold values from 0 to 128, as said below
- page_table: int32 [128], P('parts'), parts along dimension 0, may hold values from 0 to 63, each once
Outputs:
- layer_out: bfloat16 [256, 8192], P(('parts', 'wide'), 'tensor'), parts along dimension 0
The draws below stay inside these ranges and needn't reach their ends.
There are 2 independent parts, one for each index of `parts`. The reference program is written for one: setup_inputs(seed, part) draws one part's arguments, and reference() takes and returns one part's arrays. A program takes and returns all parts, laid end to end along the dimension named above; an argument that names none is the same for every part. Nothing has to cross between parts.
Inputs may be any that keep to these rules, and one draw needn't show every extreme that they name: row_adapter never falls along the rows and takes exactly 8 distinct values; its runs of equal values are the segments. block_first never falls; a segment that starts at row s and holds l rows owns the entries s, s + 128, s + 256 and so on, ceil(l / 128) of them, in order of segments; all later entries equal 128, and there is at least one such entry. `page_table`: every page is named once; page p lies on index p // 8 of wide.
All inputs are finite; a program needn't handle non-finite values.
Results may differ from the reference program's by a relative error of at most 0.0053.
Values may be sent and summed in bfloat16 or wider, within the bound.
No kernel may reach another device: no remote copies, remote signals or barrier semaphores. Data moves between devices by JAX's collectives and lax.ppermute only.
A program may use at most 128 MiB of HBM per device.

```python
import jax
import jax.numpy as jnp
from jax import lax

D = 8192
FF = 16384
R = 16
BLOCK = 128
SEGS = 8
ROWS_DEV = 16
ROWS = 128
ADAPTERS = 64
NBLK = 10
N_WIDE = 8


def segment_bounds(key):
    cut_order = jax.random.permutation(jax.random.fold_in(key, 101), ROWS - 1).astype(jnp.int32)
    cuts = jnp.sort(cut_order[:SEGS - 1] + 1)
    return jnp.concatenate([jnp.zeros((1,), jnp.int32), cuts, jnp.full((1,), ROWS, jnp.int32)])


def draw_row_adapter(key, part):
    bounds = segment_bounds(key)
    key = jax.random.fold_in(key, 7)
    inner = jax.random.permutation(key, ADAPTERS - 2).astype(jnp.int32)[:SEGS - 2] + 1
    chosen = jnp.sort(jnp.concatenate([jnp.zeros((1,), jnp.int32), inner, jnp.full((1,), ADAPTERS - 1, jnp.int32)]))
    positions = lax.iota(jnp.int32, ROWS)
    segment = jnp.sum((positions[:, None] >= bounds[None, 1:SEGS]).astype(jnp.int32), axis=1)
    return chosen[segment]


def draw_block_first(key, part):
    bounds = segment_bounds(key)
    lengths = bounds[1:] - bounds[:-1]
    counts = (lengths + BLOCK - 1) // BLOCK
    ends = jnp.cumsum(counts).astype(jnp.int32)
    labels = lax.iota(jnp.int32, NBLK)
    segment = jnp.sum((labels[:, None] >= ends[None, :]).astype(jnp.int32), axis=1)
    safe = jnp.minimum(segment, SEGS - 1)
    within = labels - (ends[safe] - counts[safe])
    opening = bounds[safe] + within * BLOCK
    return jnp.where(segment < SEGS, opening, ROWS).astype(jnp.int32)


def block_levels(key, extent, pieces, low, top_value):
    gain, own = 1.0, jax.random.fold_in(key, 6)
    for axis_at, shards_of in pieces:
        steps = jnp.exp(jax.random.uniform(jax.random.fold_in(own, axis_at), (shards_of,), jnp.float32, low / len(pieces), top_value / len(pieces)))
        gain = gain * jnp.repeat(steps, extent[axis_at] // shards_of).reshape([-1 if axis == axis_at else 1 for axis in range(len(extent))])
    return gain


def gaussian(stream_key, dims, spread, limit, shards=(), kind=jnp.bfloat16):
    array = spread * jax.random.normal(stream_key, dims, jnp.float32)
    if shards:
        array = array * block_levels(stream_key, dims, shards, -0.22, 0.18)
    return jnp.clip(array, -limit, limit).astype(kind)


def setup_inputs(seed: int = 0, part: int = 0) -> dict:
    streams_of = jax.random.split(jax.random.key(seed), 10)
    own_keys = jax.random.split(jax.random.fold_in(streams_of[9], part), 10)
    return {
        "tokens": gaussian(own_keys[0], (ROWS, D), 1.0, 6.0, ((0, 8), (1, 2))),
        "gate_weight": gaussian(streams_of[1], (D, FF), D ** -0.5, 0.0625, ((0, 2), (1, 8))),
        "up_weight": gaussian(streams_of[2], (D, FF), D ** -0.5, 0.0625, ((0, 2), (1, 8))),
        "down_weight": gaussian(streams_of[3], (FF, D), FF ** -0.5, 0.046875, ((0, 8), (1, 2))),
        "adapter_down": gaussian(own_keys[4], (ADAPTERS, R, FF), FF ** -0.5, 0.046875, ((2, 8),)),
        "adapter_up": gaussian(own_keys[5], (ADAPTERS, R, D), R ** -0.5, 1.5, ((0, 8), (2, 2))),
        "row_adapter": draw_row_adapter(jax.random.fold_in(jax.random.fold_in(streams_of[9], part), 71), part),
        "block_first": draw_block_first(jax.random.fold_in(jax.random.fold_in(streams_of[9], part), 71), part),
        "page_table": jax.random.permutation(own_keys[8], ADAPTERS).astype(jnp.int32),
    }


def shrink_rows_all(hidden, adapter_down, row_adapter, block_first):
    padded = jnp.concatenate([hidden, jnp.zeros((BLOCK, FF), hidden.dtype)], axis=0)
    marked = jnp.concatenate([row_adapter, jnp.full((BLOCK,), -1, jnp.int32)], axis=0)

    def one_block(totals, opening):
        adapter = row_adapter[jnp.minimum(opening, ROWS - 1)]
        keeping = lax.dynamic_slice_in_dim(marked, opening, BLOCK) == adapter
        window = lax.dynamic_slice_in_dim(padded, opening, BLOCK, 0)
        window = jnp.where(keeping[:, None], window, jnp.zeros((), window.dtype))
        term = lax.dot_general(window, adapter_down[adapter], (((1,), (1,)), ((), ())), preferred_element_type=jnp.float32)
        before = lax.dynamic_slice_in_dim(totals, opening, BLOCK, 0)
        return lax.dynamic_update_slice_in_dim(totals, before + term, opening, 0), None

    totals, _ = lax.scan(one_block, jnp.zeros((ROWS + BLOCK, R), jnp.float32), block_first)
    return totals[:ROWS]


def reference(tokens, gate_weight, up_weight, down_weight, adapter_down, adapter_up, row_adapter, block_first, page_table):
    gate = jnp.dot(tokens, gate_weight, preferred_element_type=jnp.float32)
    up = jnp.dot(tokens, up_weight, preferred_element_type=jnp.float32)
    hidden = (jax.nn.silu(gate) * up).astype(jnp.bfloat16)
    shrunk = shrink_rows_all(hidden, adapter_down, row_adapter, block_first).astype(jnp.bfloat16)
    row_page = page_table[row_adapter]

    def expand_rows(pair):
        shrunk_rows, page_rows = pair
        pages = adapter_up[page_rows].astype(jnp.float32)
        return jnp.einsum("rk,rkd->rd", shrunk_rows.astype(jnp.float32), pages)

    delta = lax.map(expand_rows, (shrunk.reshape(N_WIDE, ROWS_DEV, R), row_page.reshape(N_WIDE, ROWS_DEV)))
    delta = delta.reshape(ROWS, D)
    base = jnp.dot(hidden, down_weight, preferred_element_type=jnp.float32)
    return (base + delta).astype(jnp.bfloat16)
```

```python
import functools

import jax
import jax.numpy as jnp
from jax import lax
from jax.experimental import pallas as pl
from jax.experimental.pallas import tpu as pltpu
from jax.sharding import PartitionSpec as P

BLOCK = 128
CHUNKS = 2
MIB = 1 << 20

SMEM = pl.BlockSpec(memory_space=pltpu.SMEM)
VMEM = pl.BlockSpec(memory_space=pltpu.VMEM)
ANY = pl.BlockSpec(memory_space=pl.ANY)


def dot(a, b, dims=((1,), (0,))):
    return lax.dot_general(a, b, (dims, ((), ())), preferred_element_type=jnp.float32)


def swap(x, axis, n, k):
    return lax.ppermute(x, axis, [(i, i ^ k) for i in range(n)])


def reorder(x, me, n, width):
    lanes = n * width
    at = lax.broadcasted_iota(jnp.int32, x.shape, 1) // width
    bit = 1
    while bit < n:
        low = (at & bit) == 0
        other = jnp.where(low, pltpu.roll(x, lanes - bit * width, 1), pltpu.roll(x, bit * width, 1))
        x = jnp.where((me & bit) != 0, other, x)
        bit *= 2
    return x


def gate_up_kernel(n, *refs):
    blocks, (gate_w, up_w, gate, up, sent, x) = refs[:n], refs[n:]
    rows = blocks[0].shape[0]

    @pl.when(pl.program_id(0) == 0)
    def _():
        for k in range(n):
            x[k * rows : (k + 1) * rows, :] = blocks[k][...]

    g = dot(x[...], gate_w[...])
    u = dot(x[...], up_w[...])
    gate[...] = g
    up[...] = u
    sent[0] = g.astype(sent.dtype)
    sent[1] = u.astype(sent.dtype)


def gate_up(blocks, gate_w, up_w, chunk):
    n, (rows, depth) = len(blocks), blocks[0].shape
    width = gate_w.shape[1] // CHUNKS
    tile = min(256, width)
    steps = width // tile
    total = n * rows
    block = pl.BlockSpec((rows, depth), lambda j: (0, 0))
    weight = pl.BlockSpec((depth, tile), lambda j: (0, chunk * steps + j))
    out = pl.BlockSpec((total, tile), lambda j: (0, j))
    return pl.pallas_call(
        functools.partial(gate_up_kernel, n),
        grid=(steps,),
        in_specs=[block] * n + [weight, weight],
        out_specs=[out, out, pl.BlockSpec((2, total, tile), lambda j: (0, 0, j))],
        out_shape=[
            jax.ShapeDtypeStruct((total, width), jnp.float32),
            jax.ShapeDtypeStruct((total, width), jnp.float32),
            jax.ShapeDtypeStruct((2, total, width), jnp.bfloat16),
        ],
        scratch_shapes=[pltpu.VMEM((total, depth), jnp.bfloat16)],
        compiler_params=pltpu.CompilerParams(vmem_limit_bytes=44 * MIB),
        cost_estimate=pl.CostEstimate(
            flops=4 * total * depth * width, bytes_accessed=4 * depth * width, transcendentals=0
        ),
        name="gate_up",
    )(*blocks, gate_w, up_w)


def block_mask(b, ids, adapters, row_adapter, block_first):
    opening = block_first[b]
    adapter = row_adapter[jnp.minimum(opening, row_adapter.shape[0] - 1)]
    inside = (ids >= opening) & (ids < opening + BLOCK) & (adapters == adapter)
    return inside, adapter


def hidden_kernel(n, row_adapter, block_first, adapters, *refs):
    gates, ups, gots = refs[:CHUNKS], refs[CHUNKS : 2 * CHUNKS], refs[2 * CHUNKS : 3 * CHUNKS]
    adapter_down, hidden, shrunk, factors, sems = refs[3 * CHUNKS :]
    count, rank = block_first.shape[0], adapter_down.shape[1]

    def copy(b):
        adapter = row_adapter[jnp.minimum(block_first[b], row_adapter.shape[0] - 1)]
        return pltpu.make_async_copy(adapter_down.at[adapter], factors.at[pl.ds(b * rank, rank)], sems.at[b])

    for b in range(count):
        copy(b).start()
    width = gates[0].shape[1]
    for c in range(CHUNKS):
        g = gates[c][...] + gots[c][0].astype(jnp.float32)
        u = ups[c][...] + gots[c][1].astype(jnp.float32)
        hidden[:, c * width : (c + 1) * width] = (g / (1.0 + jnp.exp(-g)) * u).astype(hidden.dtype)
    for b in range(count):
        copy(b).wait()
    terms = dot(factors[...], hidden[...], ((1,), (1,)))
    total = jnp.zeros((rank, terms.shape[1]), jnp.float32)
    me = lax.axis_index("wide")
    rows = terms.shape[1] // n
    terms = reorder(terms, me, n, rows)
    ids = lax.broadcasted_iota(jnp.int32, (1, terms.shape[1]), 1)
    for b in range(count):
        inside, _ = block_mask(b, ids, adapters[...], row_adapter, block_first)
        total = total + jnp.where(inside, terms[b * rank : (b + 1) * rank], 0.0)
    shrunk[...] = total


def make_hidden(n, row_adapter, block_first, gates, ups, gots, adapter_down):
    total, width = gates[0].shape
    rank, hidden_local = adapter_down.shape[1], adapter_down.shape[2]
    count = block_first.shape[0]
    return pl.pallas_call(
        functools.partial(hidden_kernel, n),
        in_specs=[SMEM, SMEM, VMEM] + [VMEM] * (3 * CHUNKS) + [ANY],
        out_specs=[VMEM, VMEM],
        out_shape=[
            jax.ShapeDtypeStruct((total, hidden_local), jnp.bfloat16),
            jax.ShapeDtypeStruct((rank, total), jnp.float32),
        ],
        scratch_shapes=[
            pltpu.VMEM((count * rank, hidden_local), jnp.bfloat16),
            pltpu.SemaphoreType.DMA((count,)),
        ],
        compiler_params=pltpu.CompilerParams(vmem_limit_bytes=32 * MIB),
        name="hidden_shrink",
    )(row_adapter, block_first, row_adapter.reshape(1, -1), *gates, *ups, *gots, adapter_down)


def down_kernel(hidden, weight, base):
    base[...] = dot(hidden[...], weight[...])


def down(hidden, weight):
    total, depth = hidden.shape
    width = weight.shape[1]
    tile = min(512, width)
    return pl.pallas_call(
        down_kernel,
        grid=(width // tile,),
        in_specs=[pl.BlockSpec((total, depth), lambda j: (0, 0)), pl.BlockSpec((depth, tile), lambda j: (0, j))],
        out_specs=pl.BlockSpec((total, tile), lambda j: (0, j)),
        out_shape=jax.ShapeDtypeStruct((total, width), jnp.float32),
        compiler_params=pltpu.CompilerParams(vmem_limit_bytes=24 * MIB),
        cost_estimate=pl.CostEstimate(
            flops=2 * total * depth * width, bytes_accessed=2 * depth * width, transcendentals=0
        ),
        name="down",
    )(hidden, weight)


def delta_kernel(n, row_adapter, block_first, page_table, adapters, shrunk, adapter_up, base, *refs):
    outs, spread = refs[:n], refs[n]
    me = lax.axis_index("wide")
    slots, rank, _ = adapter_up.shape
    total = shrunk.shape[1]
    rows = total // n
    ids = lax.broadcasted_iota(jnp.int32, (1, total), 1)
    slot_of = jnp.full((1, total), -1, jnp.int32)
    for b in range(block_first.shape[0]):
        inside, adapter = block_mask(b, ids, adapters[...], row_adapter, block_first)
        slot_of = jnp.where(inside, page_table[adapter] - me * slots, slot_of)
    mine = shrunk[...].astype(jnp.bfloat16).astype(jnp.float32)
    for s in range(slots):
        part = reorder(jnp.where(slot_of == s, mine, 0.0), me, n, rows)
        spread[:, s * rank : (s + 1) * rank] = part.T.astype(jnp.bfloat16)
    up = adapter_up[...].reshape(slots * rank, adapter_up.shape[2])
    result = base[...] + dot(spread[...], up)
    for k in range(n):
        outs[k][...] = result[k * rows : (k + 1) * rows].astype(outs[k].dtype)


def add_delta(n, row_adapter, block_first, page_table, shrunk, adapter_up, base):
    total, width = base.shape
    slots, rank, _ = adapter_up.shape
    rows = total // n
    tile = min(1024, width)
    whole = lambda shape: pl.BlockSpec(shape, lambda j: (0,) * len(shape))
    return pl.pallas_call(
        functools.partial(delta_kernel, n),
        grid=(width // tile,),
        in_specs=[
            SMEM,
            SMEM,
            SMEM,
            whole((1, total)),
            whole((rank, total)),
            pl.BlockSpec((slots, rank, tile), lambda j: (0, 0, j)),
            pl.BlockSpec((total, tile), lambda j: (0, j)),
        ],
        out_specs=[pl.BlockSpec((rows, tile), lambda j: (0, j))] * n,
        out_shape=[jax.ShapeDtypeStruct((rows, width), jnp.bfloat16)] * n,
        scratch_shapes=[pltpu.VMEM((total, slots * rank), jnp.bfloat16)],
        compiler_params=pltpu.CompilerParams(vmem_limit_bytes=32 * MIB),
        name="add_delta",
    )(row_adapter, block_first, page_table, row_adapter.reshape(1, -1), shrunk, adapter_up, base)


def sum_kernel(*refs):
    terms, out = refs[:-1], refs[-1]
    total = terms[0][...].astype(jnp.float32)
    for term in terms[1:]:
        total = total + term[...].astype(jnp.float32)
    out[...] = total.astype(out.dtype)


def add_up(terms):
    return pl.pallas_call(
        sum_kernel,
        in_specs=[VMEM] * len(terms),
        out_specs=VMEM,
        out_shape=jax.ShapeDtypeStruct(terms[0].shape, jnp.bfloat16),
        compiler_params=pltpu.CompilerParams(vmem_limit_bytes=24 * MIB),
        name="sum_rows",
    )(*terms)


def local(
    n,
    tokens,
    gate_weight,
    up_weight,
    down_weight,
    adapter_down,
    adapter_up,
    row_adapter,
    block_first,
    page_table,
):
    far_first = list(range(n - 1, 0, -1))
    blocks = [tokens] + [None] * (n - 1)
    for k in far_first:
        blocks[k] = swap(tokens, "wide", n, k)
    gates, ups, gots = [], [], []
    for c in range(CHUNKS):
        gate, up, sent = gate_up(blocks, gate_weight, up_weight, c)
        gates.append(gate)
        ups.append(up)
        gots.append(swap(sent, "tensor", 2, 1))
    hidden, shrunk = make_hidden(n, row_adapter, block_first, gates, ups, gots, adapter_down)
    base = down(hidden, down_weight)
    bit = 1
    while bit < n:
        shrunk = shrunk + swap(shrunk, "wide", n, bit)
        bit *= 2
    parts = add_delta(n, row_adapter, block_first, page_table, shrunk, adapter_up, base)
    terms = [parts[0]] + [swap(parts[k], "wide", n, k) for k in far_first]
    return add_up(terms)


def solution(mesh):
    in_specs = (
        P(("parts", "wide"), "tensor"),
        P("tensor", "wide"),
        P("tensor", "wide"),
        P("wide", "tensor"),
        P("parts", None, "wide"),
        P(("parts", "wide"), None, "tensor"),
        P("parts"),
        P("parts"),
        P("parts"),
    )
    out_specs = P(("parts", "wide"), "tensor")
    body = functools.partial(local, mesh.shape["wide"])
    return jax.shard_map(body, mesh=mesh, in_specs=in_specs, out_specs=out_specs, check_vma=False)
```

```python
import functools

import jax
import jax.numpy as jnp
from jax import lax
from jax.experimental import pallas as pl
from jax.experimental.pallas import tpu as pltpu
from jax.sharding import PartitionSpec as P

BLOCK = 128
LIMIT = 6
MIB = 1 << 20

SMEM = pl.BlockSpec(memory_space=pltpu.SMEM)
VMEM = pl.BlockSpec(memory_space=pltpu.VMEM)
ANY = pl.BlockSpec(memory_space=pl.ANY)
HBM = pl.BlockSpec(memory_space=pltpu.HBM)


def dot(a, b, dims=((1,), (0,))):
    return lax.dot_general(a, b, (dims, ((), ())), preferred_element_type=jnp.float32)


def swap(x, axis, n, k):
    return lax.ppermute(x, axis, [(i, i ^ k) for i in range(n)])


def reorder(x, me, n, width):
    lanes = n * width
    at = lax.broadcasted_iota(jnp.int32, x.shape, 1) // width
    bit = 1
    while bit < n:
        low = (at & bit) == 0
        other = jnp.where(low, pltpu.roll(x, lanes - bit * width, 1), pltpu.roll(x, bit * width, 1))
        x = jnp.where((me & bit) != 0, other, x)
        bit *= 2
    return x


def stay(x):
    return pltpu.with_memory_space_constraint(x, pltpu.HBM)


def half_columns(width, other):
    half = lax.axis_index("tensor")
    start = ((1 - half) if other else half) * width
    return pl.ds(pl.multiple_of(start, 128), width)


def copies(source, out, columns, sems, steps=4):
    rows = out.shape[0] // steps
    parts = [pl.ds(i * rows, rows) for i in range(steps)]
    return [
        pltpu.make_async_copy(source.at[part, columns], out.at[part], sems.at[i]) for i, part in enumerate(parts)
    ]


def weight_moves(weight, sent, kept, sems):
    width = sent.shape[1]
    return copies(weight, sent, half_columns(width, True), sems.at[0]) + copies(
        weight, kept, half_columns(width, False), sems.at[1]
    )


def gate_fetch_kernel(weight, adapter_up, sent, kept, up_x, up_z, sems, up_sems):
    width = up_x.shape[2]
    moves = weight_moves(weight, sent, kept, sems)
    for h, out in enumerate((up_x, up_z)):
        moves.append(pltpu.make_async_copy(adapter_up.at[:, :, pl.ds(h * width, width)], out, up_sems.at[h]))
    for move in moves:
        move.start()
    for move in moves:
        move.wait()


def fetch_gate(weight, adapter_up):
    depth, width = weight.shape
    half = jax.ShapeDtypeStruct((depth, width // 2), weight.dtype)
    slots, rank, out_width = adapter_up.shape
    pages = jax.ShapeDtypeStruct((slots, rank, out_width // 2), adapter_up.dtype)
    return pl.pallas_call(
        gate_fetch_kernel,
        in_specs=[HBM, HBM],
        out_specs=[VMEM] * 4,
        out_shape=[half, half, pages, pages],
        scratch_shapes=[pltpu.SemaphoreType.DMA((2, 4)), pltpu.SemaphoreType.DMA((2,))],
        compiler_params=pltpu.CompilerParams(vmem_limit_bytes=LIMIT * MIB),
        cost_estimate=pl.CostEstimate(flops=0, bytes_accessed=2 * weight.size, transcendentals=0),
        name="fetch_gate",
    )(stay(weight), stay(adapter_up))


def up_fetch_kernel(row_adapter, block_first, after, weight, adapter_down, sent, kept, factors, sems, block_sems):
    count, rank = block_first.shape[0], adapter_down.shape[1]
    moves = weight_moves(weight, sent, kept, sems)
    for b in range(count):
        adapter = row_adapter[jnp.minimum(block_first[b], row_adapter.shape[0] - 1)]
        place = factors.at[pl.ds(b * rank, rank)]
        moves.append(pltpu.make_async_copy(adapter_down.at[adapter], place, block_sems.at[b]))
    for move in moves:
        move.start()
    for move in moves:
        move.wait()


def fetch_up(row_adapter, block_first, after, weight, adapter_down):
    depth, width = weight.shape
    half = jax.ShapeDtypeStruct((depth, width // 2), weight.dtype)
    count, (_, rank, hidden_local) = block_first.shape[0], adapter_down.shape
    return pl.pallas_call(
        up_fetch_kernel,
        in_specs=[SMEM, SMEM, ANY, HBM, HBM],
        out_specs=[VMEM] * 3,
        out_shape=[half, half, jax.ShapeDtypeStruct((count * rank, hidden_local), adapter_down.dtype)],
        scratch_shapes=[pltpu.SemaphoreType.DMA((2, 4)), pltpu.SemaphoreType.DMA((count,))],
        compiler_params=pltpu.CompilerParams(vmem_limit_bytes=LIMIT * MIB),
        cost_estimate=pl.CostEstimate(flops=0, bytes_accessed=0, transcendentals=0),
        name="fetch_up",
    )(row_adapter, block_first, after, stay(weight), stay(adapter_down))


def multiply(x, gate, up, out):
    width = out.shape[2]
    tile = min(256, width)
    for j in range(0, width, tile):
        out[0, :, j : j + tile] = dot(x[...], gate[:, j : j + tile])
        out[1, :, j : j + tile] = dot(x[...], up[:, j : j + tile])


def gate_up_kernel(n, *refs):
    xs, (gate, up, out, *rest) = refs[:n], refs[n:]
    x = xs[0]
    if rest:
        (x,) = rest
        rows = xs[0].shape[0]
        for k in range(n):
            x[k * rows : (k + 1) * rows, :] = xs[k][...]
    multiply(x, gate, up, out)


def gate_up(xs, gate, up):
    total, (depth, width) = sum(x.shape[0] for x in xs), gate.shape
    out = [jax.ShapeDtypeStruct((2, total, width), jnp.float32)]
    if len(xs) > 1:
        out.append(jax.ShapeDtypeStruct((total, depth), jnp.bfloat16))
    return pl.pallas_call(
        functools.partial(gate_up_kernel, len(xs)),
        in_specs=[VMEM] * (len(xs) + 2),
        out_specs=[VMEM] * len(out),
        out_shape=out,
        compiler_params=pltpu.CompilerParams(vmem_limit_bytes=LIMIT * MIB),
        cost_estimate=pl.CostEstimate(flops=0, bytes_accessed=0, transcendentals=0),
        name="gate_up",
    )(*xs, gate, up)


def silu_kernel(kept, got, hidden):
    step = 16

    @pl.loop(0, hidden.shape[0] // step)
    def _(i):
        rows = pl.ds(pl.multiple_of(i * step, step), step)
        g = kept[0, rows] + got[0, rows]
        u = kept[1, rows] + got[1, rows]
        hidden[rows] = (g / (1.0 + jnp.exp(-g)) * u).astype(hidden.dtype)


def silu(kept, got):
    return pl.pallas_call(
        silu_kernel,
        in_specs=[VMEM, VMEM],
        out_specs=VMEM,
        out_shape=jax.ShapeDtypeStruct(kept.shape[1:], jnp.bfloat16),
        compiler_params=pltpu.CompilerParams(vmem_limit_bytes=LIMIT * MIB),
        cost_estimate=pl.CostEstimate(flops=0, bytes_accessed=0, transcendentals=0),
        name="silu",
    )(kept, got)


def block_mask(b, ids, adapters, row_adapter, block_first):
    opening = block_first[b]
    adapter = row_adapter[jnp.minimum(opening, row_adapter.shape[0] - 1)]
    inside = (ids >= opening) & (ids < opening + BLOCK) & (adapters == adapter)
    return inside, adapter


def shrink_kernel(n, row_adapter, block_first, adapters, mine, other, factors, shrunk):
    count = block_first.shape[0]
    rank = factors.shape[0] // count
    width = mine.shape[1]
    half = lax.axis_index("tensor")
    first = pl.ds(pl.multiple_of(half * width, 128), width)
    second = pl.ds(pl.multiple_of((1 - half) * width, 128), width)
    terms = dot(factors[:, first], mine[...], ((1,), (1,))) + dot(factors[:, second], other[...], ((1,), (1,)))
    total = jnp.zeros((rank, terms.shape[1]), jnp.float32)
    me = lax.axis_index("wide")
    rows = terms.shape[1] // n
    terms = reorder(terms, me, n, rows)
    ids = lax.broadcasted_iota(jnp.int32, (1, terms.shape[1]), 1)
    for b in range(count):
        inside, _ = block_mask(b, ids, adapters[...], row_adapter, block_first)
        total = total + jnp.where(inside, terms[b * rank : (b + 1) * rank], 0.0)
    shrunk[...] = total


def shrink(n, row_adapter, block_first, mine, other, factors):
    total = mine.shape[0]
    count = block_first.shape[0]
    return pl.pallas_call(
        functools.partial(shrink_kernel, n),
        in_specs=[SMEM, SMEM, VMEM, VMEM, VMEM, VMEM],
        out_specs=VMEM,
        out_shape=jax.ShapeDtypeStruct((factors.shape[0] // count, total), jnp.float32),
        compiler_params=pltpu.CompilerParams(vmem_limit_bytes=LIMIT * MIB),
        cost_estimate=pl.CostEstimate(flops=0, bytes_accessed=0, transcendentals=0),
        name="shrink",
    )(row_adapter, block_first, row_adapter.reshape(1, -1), mine, other, factors)


def relays(n):
    plan = []
    for mask in (1, 2):
        plan.append((mask, [k for k in range(1, n) if k & mask and k != mask], [k for k in range(1, n) if not k & mask]))
    return plan


def down_kernel(n, h, mine, other, weight, base, raw, tiles, sems):
    total, depth = mine.shape
    rows = total // n
    half = lax.axis_index("tensor")
    first = pl.ds(pl.multiple_of(half * depth, 128), depth)
    second = pl.ds(pl.multiple_of((1 - half) * depth, 128), depth)
    count, _, tile = tiles.shape
    width = count * tile

    def copy(j):
        return pltpu.make_async_copy(weight.at[:, pl.ds(h * width + j * tile, tile)], tiles.at[j], sems.at[j])

    for j in range(count):
        copy(j).start()
    for j in range(count):
        copy(j).wait()
        columns = slice(j * tile, (j + 1) * tile)
        result = dot(mine[...], tiles[j, first]) + dot(other[...], tiles[j, second])
        base[:, columns] = result
        for i, k in enumerate(relays(n)[h][1]):
            raw[i * rows : (i + 1) * rows, columns] = result[k * rows : (k + 1) * rows].astype(raw.dtype)


def down(n, h, mine, other, weight):
    total, depth = mine.shape
    width = weight.shape[1] // 2
    tile = min(512, width)
    sent = relays(n)[h][1]
    return pl.pallas_call(
        functools.partial(down_kernel, n, h),
        in_specs=[VMEM, VMEM, HBM],
        out_specs=[VMEM] * 2,
        out_shape=[
            jax.ShapeDtypeStruct((total, width), jnp.float32),
            jax.ShapeDtypeStruct((len(sent) * total // n, width), jnp.bfloat16),
        ],
        scratch_shapes=[
            pltpu.VMEM((width // tile, 2 * depth, tile), weight.dtype),
            pltpu.SemaphoreType.DMA((width // tile,)),
        ],
        compiler_params=pltpu.CompilerParams(vmem_limit_bytes=(LIMIT + 8) * MIB),
        cost_estimate=pl.CostEstimate(flops=0, bytes_accessed=0, transcendentals=0),
        name="down",
    )(mine, other, stay(weight))


def kept_blocks(n):
    (_, _, one), (_, _, two) = relays(n)
    whole = [k for k in range(n) if k < 3 or (k in one and k in two)]
    halves = [[k for k in kept if k not in whole] for kept in (one, two)]
    return whole, halves


def delta_kernel(n, row_adapter, block_first, page_table, adapters, shrunk, up_x, up_z, next_x, next_z, base_x, base_z, *refs):
    refs = list(refs)
    plan = relays(n)
    whole, halves = kept_blocks(n)
    raws = [refs.pop(0) for _ in plan]
    places = [{k ^ mask: i for i, k in enumerate(sent)} for mask, sent, _ in plan]
    full = {k: refs.pop(0) for k in whole}
    part = [{k: refs.pop(0) for k in ks} for ks in halves]
    (spread,) = refs
    me = lax.axis_index("wide")
    slots, rank, _ = up_x.shape
    width = 2 * base_x.shape[1]
    total = shrunk.shape[1]
    rows = total // n
    ids = lax.broadcasted_iota(jnp.int32, (1, total), 1)
    page = jnp.full((1, total), -1, jnp.int32)
    for b in range(block_first.shape[0]):
        inside, adapter = block_mask(b, ids, adapters[...], row_adapter, block_first)
        page = jnp.where(inside, page_table[adapter], page)
    page = reorder(page, me, n, rows)
    mine = reorder(shrunk[...].astype(jnp.bfloat16).astype(jnp.float32), me, n, rows)
    block = ids // rows
    size = slots * rank
    for s in range(slots):
        own = page == me * slots + s
        spread[s * rank : (s + 1) * rank] = jnp.where(own, mine, 0.0)
        for h, (mask, _, _) in enumerate(plan):
            near = (page == (me ^ mask) * slots + s) & (block > 0) & ((block & mask) == 0)
            at = (h + 1) * size + s * rank
            spread[at : at + rank] = jnp.where(near, mine, 0.0)
    factor = spread[...].T.astype(jnp.bfloat16)
    tile = min(1024, width // 2)
    for h, (base, ups, near) in enumerate(((base_x, up_x, next_x), (base_z, up_z, next_z))):
        for j in range(0, width // 2, tile):
            local = slice(j, j + tile)
            columns = slice(h * (width // 2) + j, h * (width // 2) + j + tile)
            result = base[:, local] + dot(factor[:, :size], ups[:, :, local].reshape(size, tile))
            result = result + dot(factor[:, (h + 1) * size : (h + 2) * size], near[:, :, local].reshape(size, tile))
            for k in whole + halves[h]:
                term = result[k * rows : (k + 1) * rows]
                if k in places[h]:
                    at = places[h][k] * rows
                    term = term + raws[h][at : at + rows, local].astype(jnp.float32)
                if k in full:
                    full[k][:, columns] = term.astype(jnp.bfloat16)
                else:
                    part[h][k][:, local] = term.astype(jnp.bfloat16)


def add_delta(n, row_adapter, block_first, page_table, shrunk, ups, nears, bases, raws):
    total, width = bases[0].shape[0], 2 * bases[0].shape[1]
    slots, rank, _ = ups[0].shape
    rows = total // n
    whole, halves = kept_blocks(n)
    block = lambda columns: jax.ShapeDtypeStruct((rows, columns), jnp.bfloat16)
    outs = pl.pallas_call(
        functools.partial(delta_kernel, n),
        in_specs=[SMEM, SMEM, SMEM] + [VMEM] * (8 + len(raws)),
        out_specs=[VMEM] * (len(whole) + len(halves[0]) + len(halves[1])),
        out_shape=[block(width)] * len(whole) + [block(width // 2)] * (len(halves[0]) + len(halves[1])),
        scratch_shapes=[pltpu.VMEM((3 * slots * rank, total), jnp.float32)],
        compiler_params=pltpu.CompilerParams(vmem_limit_bytes=LIMIT * MIB),
        name="add_delta",
    )(
        row_adapter, block_first, page_table, row_adapter.reshape(1, -1), shrunk, *ups, *nears, *bases, *raws,
    )
    return outs[: len(whole)], outs[len(whole) : len(whole) + len(halves[0])], outs[len(whole) + len(halves[0]) :]


def sum_kernel(count, *refs):
    wholes, parts, out = refs[: count[0]], refs[count[0] : -1], refs[-1]
    width = out.shape[1] // 2
    for h in range(2):
        columns = slice(h * width, (h + 1) * width)
        total = wholes[0][:, columns].astype(jnp.float32)
        for term in wholes[1:]:
            total = total + term[:, columns].astype(jnp.float32)
        for term in parts[: count[1]] if h == 0 else parts[count[1] :]:
            total = total + term[...].astype(jnp.float32)
        out[:, columns] = total.astype(out.dtype)


def add_up(wholes, firsts, seconds):
    return pl.pallas_call(
        functools.partial(sum_kernel, (len(wholes), len(firsts))),
        in_specs=[VMEM] * (len(wholes) + len(firsts) + len(seconds)),
        out_specs=VMEM,
        out_shape=jax.ShapeDtypeStruct(wholes[0].shape, jnp.bfloat16),
        compiler_params=pltpu.CompilerParams(vmem_limit_bytes=LIMIT * MIB),
        name="sum_rows",
    )(*wholes, *firsts, *seconds)


def plus_kernel(a, b, out):
    out[...] = a[...] + b[...]


def plus(a, b):
    return pl.pallas_call(
        plus_kernel,
        in_specs=[VMEM, VMEM],
        out_specs=VMEM,
        out_shape=jax.ShapeDtypeStruct(a.shape, a.dtype),
        compiler_params=pltpu.CompilerParams(vmem_limit_bytes=LIMIT * MIB),
        cost_estimate=pl.CostEstimate(flops=0, bytes_accessed=0, transcendentals=0),
        name="plus",
    )(a, b)


def local(
    n,
    tokens,
    gate_weight,
    up_weight,
    down_weight,
    adapter_down,
    adapter_up,
    row_adapter,
    block_first,
    page_table,
):
    blocks = [tokens] + [None] * (n - 1)
    far = [k for k in range(4, n) if k % 2 == 0]
    for k in far + [1, 2, 3]:
        blocks[k] = swap(tokens, "wide", n, k)
    gate_sent, gate_kept, *ups = fetch_gate(gate_weight, adapter_up)
    last = far[-1]
    blocks[last], *ups = lax.optimization_barrier((blocks[last], *ups))
    for k in far:
        blocks[k ^ 1] = swap(blocks[k], "wide", n, 1)
    blocks[last], *blocks[1:4] = lax.optimization_barrier((blocks[last], *blocks[1:4]))
    up_sent, up_kept, factors = fetch_up(row_adapter, block_first, blocks[last], up_weight, adapter_down)
    sent, x = gate_up(blocks, gate_sent, up_sent)
    got = swap(sent, "tensor", 2, 1)
    nears = [swap(piece, "wide", n, mask) for piece, (mask, _, _) in zip(ups, relays(n))]
    (kept,) = gate_up([x], gate_kept, up_kept)
    mine = silu(kept, got)
    other = swap(mine, "tensor", 2, 1)
    shrunk = shrink(n, row_adapter, block_first, mine, other, factors)
    arrived = swap(shrunk, "wide", n, 1)
    shrunk, mine = lax.optimization_barrier((shrunk, mine))
    bases, raws = [], []
    for h in range(2):
        base, raw = down(n, h, mine, other, down_weight)
        mine, base, raw = lax.optimization_barrier((mine, base, raw))
        bases.append(base)
        raws.append(raw)
    arrived, *rest = lax.optimization_barrier((arrived, *bases, *raws, *nears))
    bases, raws, nears = rest[:2], rest[2:4], rest[4:]
    shrunk = plus(shrunk, arrived)
    raws = [swap(raw, "wide", n, mask) for raw, (mask, _, _) in zip(raws, relays(n))]
    bit = 2
    while bit < n:
        shrunk = plus(shrunk, swap(shrunk, "wide", n, bit))
        bit *= 2
    parts = add_delta(n, row_adapter, block_first, page_table, shrunk, ups, nears, bases, raws)
    whole, halves = kept_blocks(n)
    arrived = {}
    for ks, xs in reversed(list(zip([whole] + halves, parts))):
        for k, block in reversed(list(zip(ks, xs))):
            arrived[k] = block if k == 0 else swap(block, "wide", n, k)
    arrived = [[arrived[k] for k in ks] for ks in [whole] + halves]
    return add_up(*arrived)


def solution(mesh):
    in_specs = (
        P(("parts", "wide"), "tensor"),
        P("tensor", "wide"),
        P("tensor", "wide"),
        P("wide", "tensor"),
        P("parts", None, "wide"),
        P(("parts", "wide"), None, "tensor"),
        P("parts"),
        P("parts"),
        P("parts"),
    )
    out_specs = P(("parts", "wide"), "tensor")
    body = functools.partial(local, mesh.shape["wide"])
    return jax.shard_map(body, mesh=mesh, in_specs=in_specs, out_specs=out_specs, check_vma=False)
```

```python
import functools

import jax
import jax.numpy as jnp
from jax import lax
from jax.experimental import pallas as pl
from jax.experimental.pallas import tpu as pltpu
from jax.sharding import PartitionSpec as P

BLOCK = 128
LIMIT = 6
MIB = 1 << 20

SMEM = pl.BlockSpec(memory_space=pltpu.SMEM)
VMEM = pl.BlockSpec(memory_space=pltpu.VMEM)
ANY = pl.BlockSpec(memory_space=pl.ANY)
HBM = pl.BlockSpec(memory_space=pltpu.HBM)


def dot(a, b, dims=((1,), (0,))):
    return lax.dot_general(a, b, (dims, ((), ())), preferred_element_type=jnp.float32)


def swap(x, axis, n, k):
    return lax.ppermute(x, axis, [(i, i ^ k) for i in range(n)])


def reorder(x, me, n, width):
    lanes = n * width
    at = lax.broadcasted_iota(jnp.int32, x.shape, 1) // width
    bit = 1
    while bit < n:
        low = (at & bit) == 0
        other = jnp.where(low, pltpu.roll(x, lanes - bit * width, 1), pltpu.roll(x, bit * width, 1))
        x = jnp.where((me & bit) != 0, other, x)
        bit *= 2
    return x


def stay(x):
    return pltpu.with_memory_space_constraint(x, pltpu.HBM)


def half_columns(width, other):
    half = lax.axis_index("tensor")
    start = ((1 - half) if other else half) * width
    return pl.ds(pl.multiple_of(start, 128), width)


def copies(source, out, columns, sems, steps=4):
    rows = out.shape[0] // steps
    parts = [pl.ds(i * rows, rows) for i in range(steps)]
    return [
        pltpu.make_async_copy(source.at[part, columns], out.at[part], sems.at[i]) for i, part in enumerate(parts)
    ]


def weight_moves(weight, sent, kept, sems):
    width = sent.shape[1]
    return copies(weight, sent, half_columns(width, True), sems.at[0]) + copies(
        weight, kept, half_columns(width, False), sems.at[1]
    )


def gate_fetch_kernel(weight, adapter_up, sent, kept, up_x, up_z, sems, up_sems):
    width = up_x.shape[2]
    moves = weight_moves(weight, sent, kept, sems)
    for h, out in enumerate((up_x, up_z)):
        moves.append(pltpu.make_async_copy(adapter_up.at[:, :, pl.ds(h * width, width)], out, up_sems.at[h]))
    for move in moves:
        move.start()
    for move in moves:
        move.wait()


def fetch_gate(weight, adapter_up):
    depth, width = weight.shape
    half = jax.ShapeDtypeStruct((depth, width // 2), weight.dtype)
    slots, rank, out_width = adapter_up.shape
    pages = jax.ShapeDtypeStruct((slots, rank, out_width // 2), adapter_up.dtype)
    return pl.pallas_call(
        gate_fetch_kernel,
        in_specs=[HBM, HBM],
        out_specs=[VMEM] * 4,
        out_shape=[half, half, pages, pages],
        scratch_shapes=[pltpu.SemaphoreType.DMA((2, 4)), pltpu.SemaphoreType.DMA((2,))],
        compiler_params=pltpu.CompilerParams(vmem_limit_bytes=LIMIT * MIB),
        cost_estimate=pl.CostEstimate(flops=0, bytes_accessed=2 * weight.size, transcendentals=0),
        name="fetch_gate",
    )(stay(weight), stay(adapter_up))


def up_fetch_kernel(row_adapter, block_first, after, weight, adapter_down, sent, kept, factors, sems, block_sems):
    count, rank = block_first.shape[0], adapter_down.shape[1]
    moves = weight_moves(weight, sent, kept, sems)
    for b in range(count):
        adapter = row_adapter[jnp.minimum(block_first[b], row_adapter.shape[0] - 1)]
        place = factors.at[pl.ds(b * rank, rank)]
        moves.append(pltpu.make_async_copy(adapter_down.at[adapter], place, block_sems.at[b]))
    for move in moves:
        move.start()
    for move in moves:
        move.wait()


def fetch_up(row_adapter, block_first, after, weight, adapter_down):
    depth, width = weight.shape
    half = jax.ShapeDtypeStruct((depth, width // 2), weight.dtype)
    count, (_, rank, hidden_local) = block_first.shape[0], adapter_down.shape
    return pl.pallas_call(
        up_fetch_kernel,
        in_specs=[SMEM, SMEM, ANY, HBM, HBM],
        out_specs=[VMEM] * 3,
        out_shape=[half, half, jax.ShapeDtypeStruct((count * rank, hidden_local), adapter_down.dtype)],
        scratch_shapes=[pltpu.SemaphoreType.DMA((2, 4)), pltpu.SemaphoreType.DMA((count,))],
        compiler_params=pltpu.CompilerParams(vmem_limit_bytes=LIMIT * MIB),
        cost_estimate=pl.CostEstimate(flops=0, bytes_accessed=0, transcendentals=0),
        name="fetch_up",
    )(row_adapter, block_first, after, stay(weight), stay(adapter_down))


def multiply(x, gate, up, out):
    width = out.shape[2]
    tile = min(256, width)
    for j in range(0, width, tile):
        out[0, :, j : j + tile] = dot(x[...], gate[:, j : j + tile])
        out[1, :, j : j + tile] = dot(x[...], up[:, j : j + tile])


def gate_up_kernel(n, *refs):
    xs, (gate, up, out, *rest) = refs[:n], refs[n:]
    x = xs[0]
    if rest:
        (x,) = rest
        rows = xs[0].shape[0]
        for k in range(n):
            x[k * rows : (k + 1) * rows, :] = xs[k][...]
    multiply(x, gate, up, out)


def gate_up(xs, gate, up):
    total, (depth, width) = sum(x.shape[0] for x in xs), gate.shape
    out = [jax.ShapeDtypeStruct((2, total, width), jnp.float32)]
    if len(xs) > 1:
        out.append(jax.ShapeDtypeStruct((total, depth), jnp.bfloat16))
    return pl.pallas_call(
        functools.partial(gate_up_kernel, len(xs)),
        in_specs=[VMEM] * (len(xs) + 2),
        out_specs=[VMEM] * len(out),
        out_shape=out,
        compiler_params=pltpu.CompilerParams(vmem_limit_bytes=LIMIT * MIB),
        cost_estimate=pl.CostEstimate(flops=0, bytes_accessed=0, transcendentals=0),
        name="gate_up",
    )(*xs, gate, up)


def silu_kernel(kept, got, hidden):
    step = 16

    @pl.loop(0, hidden.shape[0] // step)
    def _(i):
        rows = pl.ds(pl.multiple_of(i * step, step), step)
        g = kept[0, rows] + got[0, rows]
        u = kept[1, rows] + got[1, rows]
        hidden[rows] = (g / (1.0 + jnp.exp(-g)) * u).astype(hidden.dtype)


def silu(kept, got):
    return pl.pallas_call(
        silu_kernel,
        in_specs=[VMEM, VMEM],
        out_specs=VMEM,
        out_shape=jax.ShapeDtypeStruct(kept.shape[1:], jnp.bfloat16),
        compiler_params=pltpu.CompilerParams(vmem_limit_bytes=LIMIT * MIB),
        cost_estimate=pl.CostEstimate(flops=0, bytes_accessed=0, transcendentals=0),
        name="silu",
    )(kept, got)


def block_mask(b, ids, adapters, row_adapter, block_first):
    opening = block_first[b]
    adapter = row_adapter[jnp.minimum(opening, row_adapter.shape[0] - 1)]
    inside = (ids >= opening) & (ids < opening + BLOCK) & (adapters == adapter)
    return inside, adapter


def shrink_kernel(n, row_adapter, block_first, adapters, mine, other, factors, shrunk):
    count = block_first.shape[0]
    rank = factors.shape[0] // count
    width = mine.shape[1]
    half = lax.axis_index("tensor")
    first = pl.ds(pl.multiple_of(half * width, 128), width)
    second = pl.ds(pl.multiple_of((1 - half) * width, 128), width)
    terms = dot(factors[:, first], mine[...], ((1,), (1,))) + dot(factors[:, second], other[...], ((1,), (1,)))
    total = jnp.zeros((rank, terms.shape[1]), jnp.float32)
    me = lax.axis_index("wide")
    rows = terms.shape[1] // n
    terms = reorder(terms, me, n, rows)
    ids = lax.broadcasted_iota(jnp.int32, (1, terms.shape[1]), 1)
    for b in range(count):
        inside, _ = block_mask(b, ids, adapters[...], row_adapter, block_first)
        total = total + jnp.where(inside, terms[b * rank : (b + 1) * rank], 0.0)
    shrunk[...] = total


def shrink(n, row_adapter, block_first, mine, other, factors):
    total = mine.shape[0]
    count = block_first.shape[0]
    return pl.pallas_call(
        functools.partial(shrink_kernel, n),
        in_specs=[SMEM, SMEM, VMEM, VMEM, VMEM, VMEM],
        out_specs=VMEM,
        out_shape=jax.ShapeDtypeStruct((factors.shape[0] // count, total), jnp.float32),
        compiler_params=pltpu.CompilerParams(vmem_limit_bytes=LIMIT * MIB),
        cost_estimate=pl.CostEstimate(flops=0, bytes_accessed=0, transcendentals=0),
        name="shrink",
    )(row_adapter, block_first, row_adapter.reshape(1, -1), mine, other, factors)


def relays(n):
    plan = []
    for mask in (1, 2):
        plan.append((mask, [k for k in range(1, n) if k & mask and k != mask], [k for k in range(1, n) if not k & mask]))
    return plan


def down_kernel(n, mine, other, weight, base_x, base_z, raw_x, raw_z, tiles, sems):
    total, depth = mine.shape
    rows = total // n
    half = lax.axis_index("tensor")
    first = pl.ds(pl.multiple_of(half * depth, 128), depth)
    second = pl.ds(pl.multiple_of((1 - half) * depth, 128), depth)
    count, _, tile = tiles.shape

    def copy(j):
        return pltpu.make_async_copy(weight.at[:, pl.ds(j * tile, tile)], tiles.at[j], sems.at[j])

    for j in range(count):
        copy(j).start()
    for j in range(count):
        copy(j).wait()
        h, at = divmod(j, count // 2)
        base, raw = ((base_x, raw_x), (base_z, raw_z))[h]
        columns = slice(at * tile, (at + 1) * tile)
        result = dot(mine[...], tiles[j, first]) + dot(other[...], tiles[j, second])
        base[:, columns] = result
        for i, k in enumerate(relays(n)[h][1]):
            raw[i * rows : (i + 1) * rows, columns] = result[k * rows : (k + 1) * rows].astype(raw.dtype)


def down(n, mine, other, weight):
    total, depth = mine.shape
    width = weight.shape[1] // 2
    tile = min(512, width)
    base = jax.ShapeDtypeStruct((total, width), jnp.float32)
    raws = [jax.ShapeDtypeStruct((len(sent) * total // n, width), jnp.bfloat16) for _, sent, _ in relays(n)]
    return pl.pallas_call(
        functools.partial(down_kernel, n),
        in_specs=[VMEM, VMEM, HBM],
        out_specs=[VMEM] * 4,
        out_shape=[base, base, *raws],
        scratch_shapes=[
            pltpu.VMEM((2 * width // tile, 2 * depth, tile), weight.dtype),
            pltpu.SemaphoreType.DMA((2 * width // tile,)),
        ],
        compiler_params=pltpu.CompilerParams(vmem_limit_bytes=(LIMIT + 16) * MIB),
        cost_estimate=pl.CostEstimate(flops=0, bytes_accessed=0, transcendentals=0),
        name="down",
    )(mine, other, stay(weight))


def kept_blocks(n):
    (_, _, one), (_, _, two) = relays(n)
    whole = [k for k in range(n) if k < 3 or (k in one and k in two)]
    halves = [[k for k in kept if k not in whole] for kept in (one, two)]
    return whole, halves


def delta_kernel(n, row_adapter, block_first, page_table, adapters, shrunk, up_x, up_z, next_x, next_z, base_x, base_z, *refs):
    refs = list(refs)
    plan = relays(n)
    whole, halves = kept_blocks(n)
    raws = [refs.pop(0) for _ in plan]
    places = [{k ^ mask: i for i, k in enumerate(sent)} for mask, sent, _ in plan]
    full = {k: refs.pop(0) for k in whole}
    part = [{k: refs.pop(0) for k in ks} for ks in halves]
    (spread,) = refs
    me = lax.axis_index("wide")
    slots, rank, _ = up_x.shape
    width = 2 * base_x.shape[1]
    total = shrunk.shape[1]
    rows = total // n
    ids = lax.broadcasted_iota(jnp.int32, (1, total), 1)
    page = jnp.full((1, total), -1, jnp.int32)
    for b in range(block_first.shape[0]):
        inside, adapter = block_mask(b, ids, adapters[...], row_adapter, block_first)
        page = jnp.where(inside, page_table[adapter], page)
    page = reorder(page, me, n, rows)
    mine = reorder(shrunk[...].astype(jnp.bfloat16).astype(jnp.float32), me, n, rows)
    block = ids // rows
    size = slots * rank
    for s in range(slots):
        own = page == me * slots + s
        spread[s * rank : (s + 1) * rank] = jnp.where(own, mine, 0.0)
        for h, (mask, _, _) in enumerate(plan):
            near = (page == (me ^ mask) * slots + s) & (block > 0) & ((block & mask) == 0)
            at = (h + 1) * size + s * rank
            spread[at : at + rank] = jnp.where(near, mine, 0.0)
    factor = spread[...].T.astype(jnp.bfloat16)
    tile = min(1024, width // 2)
    for h, (base, ups, near) in enumerate(((base_x, up_x, next_x), (base_z, up_z, next_z))):
        for j in range(0, width // 2, tile):
            local = slice(j, j + tile)
            columns = slice(h * (width // 2) + j, h * (width // 2) + j + tile)
            result = base[:, local] + dot(factor[:, :size], ups[:, :, local].reshape(size, tile))
            result = result + dot(factor[:, (h + 1) * size : (h + 2) * size], near[:, :, local].reshape(size, tile))
            for k in whole + halves[h]:
                term = result[k * rows : (k + 1) * rows]
                if k in places[h]:
                    at = places[h][k] * rows
                    term = term + raws[h][at : at + rows, local].astype(jnp.float32)
                if k in full:
                    full[k][:, columns] = term.astype(jnp.bfloat16)
                else:
                    part[h][k][:, local] = term.astype(jnp.bfloat16)


def add_delta(n, row_adapter, block_first, page_table, shrunk, ups, nears, bases, raws):
    total, width = bases[0].shape[0], 2 * bases[0].shape[1]
    slots, rank, _ = ups[0].shape
    rows = total // n
    whole, halves = kept_blocks(n)
    block = lambda columns: jax.ShapeDtypeStruct((rows, columns), jnp.bfloat16)
    outs = pl.pallas_call(
        functools.partial(delta_kernel, n),
        in_specs=[SMEM, SMEM, SMEM] + [VMEM] * (8 + len(raws)),
        out_specs=[VMEM] * (len(whole) + len(halves[0]) + len(halves[1])),
        out_shape=[block(width)] * len(whole) + [block(width // 2)] * (len(halves[0]) + len(halves[1])),
        scratch_shapes=[pltpu.VMEM((3 * slots * rank, total), jnp.float32)],
        compiler_params=pltpu.CompilerParams(vmem_limit_bytes=LIMIT * MIB),
        name="add_delta",
    )(
        row_adapter, block_first, page_table, row_adapter.reshape(1, -1), shrunk, *ups, *nears, *bases, *raws,
    )
    return outs[: len(whole)], outs[len(whole) : len(whole) + len(halves[0])], outs[len(whole) + len(halves[0]) :]


def sum_kernel(count, *refs):
    wholes, parts, out = refs[: count[0]], refs[count[0] : -1], refs[-1]
    width = out.shape[1] // 2
    for h in range(2):
        columns = slice(h * width, (h + 1) * width)
        total = wholes[0][:, columns].astype(jnp.float32)
        for term in wholes[1:]:
            total = total + term[:, columns].astype(jnp.float32)
        for term in parts[: count[1]] if h == 0 else parts[count[1] :]:
            total = total + term[...].astype(jnp.float32)
        out[:, columns] = total.astype(out.dtype)


def add_up(wholes, firsts, seconds):
    return pl.pallas_call(
        functools.partial(sum_kernel, (len(wholes), len(firsts))),
        in_specs=[VMEM] * (len(wholes) + len(firsts) + len(seconds)),
        out_specs=VMEM,
        out_shape=jax.ShapeDtypeStruct(wholes[0].shape, jnp.bfloat16),
        compiler_params=pltpu.CompilerParams(vmem_limit_bytes=LIMIT * MIB),
        name="sum_rows",
    )(*wholes, *firsts, *seconds)


def plus_kernel(a, b, out):
    out[...] = a[...] + b[...]


def plus(a, b):
    return pl.pallas_call(
        plus_kernel,
        in_specs=[VMEM, VMEM],
        out_specs=VMEM,
        out_shape=jax.ShapeDtypeStruct(a.shape, a.dtype),
        compiler_params=pltpu.CompilerParams(vmem_limit_bytes=LIMIT * MIB),
        cost_estimate=pl.CostEstimate(flops=0, bytes_accessed=0, transcendentals=0),
        name="plus",
    )(a, b)


def local(
    n,
    tokens,
    gate_weight,
    up_weight,
    down_weight,
    adapter_down,
    adapter_up,
    row_adapter,
    block_first,
    page_table,
):
    blocks = [tokens] + [None] * (n - 1)
    far = [k for k in range(4, n) if k % 2 == 0]
    for k in far + [1, 2, 3]:
        blocks[k] = swap(tokens, "wide", n, k)
    gate_sent, gate_kept, *ups = fetch_gate(gate_weight, adapter_up)
    last = far[-1]
    blocks[last], *ups = lax.optimization_barrier((blocks[last], *ups))
    for k in far:
        blocks[k ^ 1] = swap(blocks[k], "wide", n, 1)
    blocks[last], *blocks[1:4] = lax.optimization_barrier((blocks[last], *blocks[1:4]))
    up_sent, up_kept, factors = fetch_up(row_adapter, block_first, blocks[last], up_weight, adapter_down)
    sent, x = gate_up(blocks, gate_sent, up_sent)
    got = swap(sent, "tensor", 2, 1)
    nears = [swap(piece, "wide", n, mask) for piece, (mask, _, _) in zip(ups, relays(n))]
    (kept,) = gate_up([x], gate_kept, up_kept)
    mine = silu(kept, got)
    other = swap(mine, "tensor", 2, 1)
    shrunk = shrink(n, row_adapter, block_first, mine, other, factors)
    arrived = swap(shrunk, "wide", n, 1)
    shrunk, mine = lax.optimization_barrier((shrunk, mine))
    *sums, raw_x, raw_z = down(n, mine, other, down_weight)
    arrived, *rest = lax.optimization_barrier((arrived, *sums, raw_x, raw_z, *nears))
    bases, raws, nears = rest[:2], rest[2:4], rest[4:]
    shrunk = plus(shrunk, arrived)
    raws[0] = swap(raws[0], "wide", n, 1)
    bit = 2
    while bit < n:
        shrunk = plus(shrunk, swap(shrunk, "wide", n, bit))
        if bit == 2:
            shrunk, raws[1] = lax.optimization_barrier((shrunk, raws[1]))
            raws[1] = swap(raws[1], "wide", n, 2)
        bit *= 2
    parts = add_delta(n, row_adapter, block_first, page_table, shrunk, ups, nears, bases, raws)
    whole, halves = kept_blocks(n)
    arrived = {}
    for ks, xs in reversed(list(zip([whole] + halves, parts))):
        for k, block in reversed(list(zip(ks, xs))):
            arrived[k] = block if k == 0 else swap(block, "wide", n, k)
    last = [k for k in arrived if k > 2]
    arrived.update(zip(last, lax.optimization_barrier([arrived[k] for k in last])))
    arrived = [[arrived[k] for k in ks] for ks in [whole] + halves]
    return add_up(*arrived)


def solution(mesh):
    in_specs = (
        P(("parts", "wide"), "tensor"),
        P("tensor", "wide"),
        P("tensor", "wide"),
        P("wide", "tensor"),
        P("parts", None, "wide"),
        P(("parts", "wide"), None, "tensor"),
        P("parts"),
        P("parts"),
        P("parts"),
    )
    out_specs = P(("parts", "wide"), "tensor")
    body = functools.partial(local, mesh.shape["wide"])
    return jax.shard_map(body, mesh=mesh, in_specs=in_specs, out_specs=out_specs, check_vma=False)
```

```python
import functools

import jax
import jax.numpy as jnp
from jax import lax
from jax.experimental import pallas as pl
from jax.experimental.pallas import tpu as pltpu
from jax.sharding import PartitionSpec as P

BLOCK = 128
LIMIT = 6
MIB = 1 << 20

SMEM = pl.BlockSpec(memory_space=pltpu.SMEM)
VMEM = pl.BlockSpec(memory_space=pltpu.VMEM)
ANY = pl.BlockSpec(memory_space=pl.ANY)
HBM = pl.BlockSpec(memory_space=pltpu.HBM)


def dot(a, b, dims=((1,), (0,))):
    return lax.dot_general(a, b, (dims, ((), ())), preferred_element_type=jnp.float32)


def swap(x, axis, n, k):
    return lax.ppermute(x, axis, [(i, i ^ k) for i in range(n)])


def reorder(x, me, n, width):
    lanes = n * width
    at = lax.broadcasted_iota(jnp.int32, x.shape, 1) // width
    bit = 1
    while bit < n:
        low = (at & bit) == 0
        other = jnp.where(low, pltpu.roll(x, lanes - bit * width, 1), pltpu.roll(x, bit * width, 1))
        x = jnp.where((me & bit) != 0, other, x)
        bit *= 2
    return x


def stay(x):
    return pltpu.with_memory_space_constraint(x, pltpu.HBM)


def half_columns(width, other):
    half = lax.axis_index("tensor")
    start = ((1 - half) if other else half) * width
    return pl.ds(pl.multiple_of(start, 128), width)


def copies(source, out, columns, sems, steps=4):
    rows = out.shape[0] // steps
    parts = [pl.ds(i * rows, rows) for i in range(steps)]
    return [
        pltpu.make_async_copy(source.at[part, columns], out.at[part], sems.at[i]) for i, part in enumerate(parts)
    ]


def weight_moves(weight, sent, kept, sems):
    width = sent.shape[1]
    return copies(weight, sent, half_columns(width, True), sems.at[0]) + copies(
        weight, kept, half_columns(width, False), sems.at[1]
    )


def kept_parts(width):
    half = width // 2
    return [half // 2] * 2 if half % 256 == 0 else [half]


def kept_columns(part, width, total):
    start = lax.axis_index("tensor") * (total // 2) + part * width
    return pl.ds(pl.multiple_of(start, 128), width)


def gate_fetch_kernel(weight, up, adapter_up, sent, kept, up_first, up_x, up_z, sems, up_sems):
    width = up_x.shape[2]
    moves = weight_moves(weight, sent, kept, sems)
    moves += copies(up, up_first, kept_columns(0, up_first.shape[1], up.shape[1]), sems.at[2])
    for h, out in enumerate((up_x, up_z)):
        moves.append(pltpu.make_async_copy(adapter_up.at[:, :, pl.ds(h * width, width)], out, up_sems.at[h]))
    for move in moves:
        move.start()
    for move in moves:
        move.wait()


def fetch_gate(weight, up, adapter_up):
    depth, width = weight.shape
    half = jax.ShapeDtypeStruct((depth, width // 2), weight.dtype)
    first = jax.ShapeDtypeStruct((depth, kept_parts(width)[0]), weight.dtype)
    slots, rank, out_width = adapter_up.shape
    pages = jax.ShapeDtypeStruct((slots, rank, out_width // 2), adapter_up.dtype)
    return pl.pallas_call(
        gate_fetch_kernel,
        in_specs=[HBM, HBM, HBM],
        out_specs=[VMEM] * 5,
        out_shape=[half, half, first, pages, pages],
        scratch_shapes=[pltpu.SemaphoreType.DMA((3, 4)), pltpu.SemaphoreType.DMA((2,))],
        compiler_params=pltpu.CompilerParams(vmem_limit_bytes=LIMIT * MIB),
        cost_estimate=pl.CostEstimate(flops=0, bytes_accessed=2 * weight.size, transcendentals=0),
        name="fetch_gate",
    )(stay(weight), stay(up), stay(adapter_up))


def up_fetch_kernel(row_adapter, block_first, after, weight, adapter_down, sent, factors, *refs):
    more, (sems, block_sems) = refs[:-2], refs[-2:]
    count, rank = block_first.shape[0], adapter_down.shape[1]
    moves = copies(weight, sent, half_columns(sent.shape[1], True), sems.at[0])
    for part, out in enumerate(more, 1):
        moves += copies(weight, out, kept_columns(part, out.shape[1], weight.shape[1]), sems.at[part])
    for b in range(count):
        adapter = row_adapter[jnp.minimum(block_first[b], row_adapter.shape[0] - 1)]
        place = factors.at[pl.ds(b * rank, rank)]
        moves.append(pltpu.make_async_copy(adapter_down.at[adapter], place, block_sems.at[b]))
    for move in moves:
        move.start()
    for move in moves:
        move.wait()


def fetch_up(row_adapter, block_first, after, weight, adapter_down):
    depth, width = weight.shape
    half = jax.ShapeDtypeStruct((depth, width // 2), weight.dtype)
    more = [jax.ShapeDtypeStruct((depth, part), weight.dtype) for part in kept_parts(width)[1:]]
    count, (_, rank, hidden_local) = block_first.shape[0], adapter_down.shape
    return pl.pallas_call(
        up_fetch_kernel,
        in_specs=[SMEM, SMEM, ANY, HBM, HBM],
        out_specs=[VMEM] * (2 + len(more)),
        out_shape=[half, jax.ShapeDtypeStruct((count * rank, hidden_local), adapter_down.dtype), *more],
        scratch_shapes=[pltpu.SemaphoreType.DMA((2, 4)), pltpu.SemaphoreType.DMA((count,))],
        compiler_params=pltpu.CompilerParams(vmem_limit_bytes=LIMIT * MIB),
        cost_estimate=pl.CostEstimate(flops=0, bytes_accessed=0, transcendentals=0),
        name="fetch_up",
    )(row_adapter, block_first, after, stay(weight), stay(adapter_down))


def multiply(x, gate, ups, out):
    width = out.shape[2]
    part = ups[0].shape[1]
    tile = min(256, width)
    for j in range(0, width, tile):
        out[0, :, j : j + tile] = dot(x[...], gate[:, j : j + tile])
        out[1, :, j : j + tile] = dot(x[...], ups[j // part][:, j % part : j % part + tile])


def gate_up_kernel(n, parts, *refs):
    xs, gate, ups, (out, *rest) = refs[:n], refs[n], refs[n + 1 : n + 1 + parts], refs[n + 1 + parts :]
    x = xs[0]
    if rest:
        (x,) = rest
        rows = xs[0].shape[0]
        for k in range(n):
            x[k * rows : (k + 1) * rows, :] = xs[k][...]
    multiply(x, gate, ups, out)


def gate_up(xs, gate, ups):
    total, (depth, width) = sum(x.shape[0] for x in xs), gate.shape
    out = [jax.ShapeDtypeStruct((2, total, width), jnp.float32)]
    if len(xs) > 1:
        out.append(jax.ShapeDtypeStruct((total, depth), jnp.bfloat16))
    return pl.pallas_call(
        functools.partial(gate_up_kernel, len(xs), len(ups)),
        in_specs=[VMEM] * (len(xs) + 1 + len(ups)),
        out_specs=[VMEM] * len(out),
        out_shape=out,
        compiler_params=pltpu.CompilerParams(vmem_limit_bytes=LIMIT * MIB),
        cost_estimate=pl.CostEstimate(flops=0, bytes_accessed=0, transcendentals=0),
        name="gate_up",
    )(*xs, gate, *ups)


def silu_kernel(kept, got, hidden):
    step = 16

    @pl.loop(0, hidden.shape[0] // step)
    def _(i):
        rows = pl.ds(pl.multiple_of(i * step, step), step)
        g = kept[0, rows] + got[0, rows]
        u = kept[1, rows] + got[1, rows]
        hidden[rows] = (g / (1.0 + jnp.exp(-g)) * u).astype(hidden.dtype)


def silu(kept, got):
    return pl.pallas_call(
        silu_kernel,
        in_specs=[VMEM, VMEM],
        out_specs=VMEM,
        out_shape=jax.ShapeDtypeStruct(kept.shape[1:], jnp.bfloat16),
        compiler_params=pltpu.CompilerParams(vmem_limit_bytes=LIMIT * MIB),
        cost_estimate=pl.CostEstimate(flops=0, bytes_accessed=0, transcendentals=0),
        name="silu",
    )(kept, got)


def block_mask(b, ids, adapters, row_adapter, block_first):
    opening = block_first[b]
    adapter = row_adapter[jnp.minimum(opening, row_adapter.shape[0] - 1)]
    inside = (ids >= opening) & (ids < opening + BLOCK) & (adapters == adapter)
    return inside, adapter


def shrink_kernel(n, row_adapter, block_first, adapters, mine, other, factors, shrunk):
    count = block_first.shape[0]
    rank = factors.shape[0] // count
    width = mine.shape[1]
    half = lax.axis_index("tensor")
    first = pl.ds(pl.multiple_of(half * width, 128), width)
    second = pl.ds(pl.multiple_of((1 - half) * width, 128), width)
    terms = dot(factors[:, first], mine[...], ((1,), (1,))) + dot(factors[:, second], other[...], ((1,), (1,)))
    total = jnp.zeros((rank, terms.shape[1]), jnp.float32)
    me = lax.axis_index("wide")
    rows = terms.shape[1] // n
    terms = reorder(terms, me, n, rows)
    ids = lax.broadcasted_iota(jnp.int32, (1, terms.shape[1]), 1)
    for b in range(count):
        inside, _ = block_mask(b, ids, adapters[...], row_adapter, block_first)
        total = total + jnp.where(inside, terms[b * rank : (b + 1) * rank], 0.0)
    shrunk[...] = total


def shrink(n, row_adapter, block_first, mine, other, factors):
    total = mine.shape[0]
    count = block_first.shape[0]
    return pl.pallas_call(
        functools.partial(shrink_kernel, n),
        in_specs=[SMEM, SMEM, VMEM, VMEM, VMEM, VMEM],
        out_specs=VMEM,
        out_shape=jax.ShapeDtypeStruct((factors.shape[0] // count, total), jnp.float32),
        compiler_params=pltpu.CompilerParams(vmem_limit_bytes=LIMIT * MIB),
        cost_estimate=pl.CostEstimate(flops=0, bytes_accessed=0, transcendentals=0),
        name="shrink",
    )(row_adapter, block_first, row_adapter.reshape(1, -1), mine, other, factors)


def relays(n):
    plan = []
    for mask in (1, 2):
        plan.append((mask, [k for k in range(1, n) if k & mask and k != mask], [k for k in range(1, n) if not k & mask]))
    return plan


def down_kernel(n, mine, other, weight, base_x, base_z, raw_x, raw_z, tiles, sems):
    total, depth = mine.shape
    rows = total // n
    half = lax.axis_index("tensor")
    first = pl.ds(pl.multiple_of(half * depth, 128), depth)
    second = pl.ds(pl.multiple_of((1 - half) * depth, 128), depth)
    count, _, tile = tiles.shape

    def copy(j):
        return pltpu.make_async_copy(weight.at[:, pl.ds(j * tile, tile)], tiles.at[j], sems.at[j])

    for j in range(count):
        copy(j).start()
    for j in range(count):
        copy(j).wait()
        h, at = divmod(j, count // 2)
        base, raw = ((base_x, raw_x), (base_z, raw_z))[h]
        columns = slice(at * tile, (at + 1) * tile)
        result = dot(mine[...], tiles[j, first]) + dot(other[...], tiles[j, second])
        base[:, columns] = result
        for i, k in enumerate(relays(n)[h][1]):
            raw[i * rows : (i + 1) * rows, columns] = result[k * rows : (k + 1) * rows].astype(raw.dtype)


def down(n, mine, other, weight):
    total, depth = mine.shape
    width = weight.shape[1] // 2
    tile = min(512, width)
    base = jax.ShapeDtypeStruct((total, width), jnp.float32)
    raws = [jax.ShapeDtypeStruct((len(sent) * total // n, width), jnp.bfloat16) for _, sent, _ in relays(n)]
    return pl.pallas_call(
        functools.partial(down_kernel, n),
        in_specs=[VMEM, VMEM, HBM],
        out_specs=[VMEM] * 4,
        out_shape=[base, base, *raws],
        scratch_shapes=[
            pltpu.VMEM((2 * width // tile, 2 * depth, tile), weight.dtype),
            pltpu.SemaphoreType.DMA((2 * width // tile,)),
        ],
        compiler_params=pltpu.CompilerParams(vmem_limit_bytes=(LIMIT + 16) * MIB),
        cost_estimate=pl.CostEstimate(flops=0, bytes_accessed=0, transcendentals=0),
        name="down",
    )(mine, other, stay(weight))


def kept_blocks(n):
    (_, _, one), (_, _, two) = relays(n)
    whole = [k for k in range(n) if k < 3 or (k in one and k in two)]
    halves = [[k for k in kept if k not in whole] for kept in (one, two)]
    return whole, halves


def delta_kernel(n, row_adapter, block_first, page_table, adapters, shrunk, up_x, up_z, next_x, next_z, base_x, base_z, *refs):
    refs = list(refs)
    plan = relays(n)
    whole, halves = kept_blocks(n)
    raws = [refs.pop(0) for _ in plan]
    places = [{k ^ mask: i for i, k in enumerate(sent)} for mask, sent, _ in plan]
    full = {k: refs.pop(0) for k in whole}
    part = [{k: refs.pop(0) for k in ks} for ks in halves]
    (spread,) = refs
    me = lax.axis_index("wide")
    slots, rank, _ = up_x.shape
    width = 2 * base_x.shape[1]
    total = shrunk.shape[1]
    rows = total // n
    ids = lax.broadcasted_iota(jnp.int32, (1, total), 1)
    page = jnp.full((1, total), -1, jnp.int32)
    for b in range(block_first.shape[0]):
        inside, adapter = block_mask(b, ids, adapters[...], row_adapter, block_first)
        page = jnp.where(inside, page_table[adapter], page)
    page = reorder(page, me, n, rows)
    mine = reorder(shrunk[...].astype(jnp.bfloat16).astype(jnp.float32), me, n, rows)
    block = ids // rows
    size = slots * rank
    for s in range(slots):
        own = page == me * slots + s
        spread[s * rank : (s + 1) * rank] = jnp.where(own, mine, 0.0)
        for h, (mask, _, _) in enumerate(plan):
            near = (page == (me ^ mask) * slots + s) & (block > 0) & ((block & mask) == 0)
            at = (h + 1) * size + s * rank
            spread[at : at + rank] = jnp.where(near, mine, 0.0)
    factor = spread[...].T.astype(jnp.bfloat16)
    tile = min(1024, width // 2)
    for h, (base, ups, near) in enumerate(((base_x, up_x, next_x), (base_z, up_z, next_z))):
        for j in range(0, width // 2, tile):
            local = slice(j, j + tile)
            columns = slice(h * (width // 2) + j, h * (width // 2) + j + tile)
            result = base[:, local] + dot(factor[:, :size], ups[:, :, local].reshape(size, tile))
            result = result + dot(factor[:, (h + 1) * size : (h + 2) * size], near[:, :, local].reshape(size, tile))
            for k in whole + halves[h]:
                term = result[k * rows : (k + 1) * rows]
                if k in places[h]:
                    at = places[h][k] * rows
                    term = term + raws[h][at : at + rows, local].astype(jnp.float32)
                if k in full:
                    full[k][:, columns] = term.astype(jnp.bfloat16)
                else:
                    part[h][k][:, local] = term.astype(jnp.bfloat16)


def add_delta(n, row_adapter, block_first, page_table, shrunk, ups, nears, bases, raws):
    total, width = bases[0].shape[0], 2 * bases[0].shape[1]
    slots, rank, _ = ups[0].shape
    rows = total // n
    whole, halves = kept_blocks(n)
    block = lambda columns: jax.ShapeDtypeStruct((rows, columns), jnp.bfloat16)
    outs = pl.pallas_call(
        functools.partial(delta_kernel, n),
        in_specs=[SMEM, SMEM, SMEM] + [VMEM] * (8 + len(raws)),
        out_specs=[VMEM] * (len(whole) + len(halves[0]) + len(halves[1])),
        out_shape=[block(width)] * len(whole) + [block(width // 2)] * (len(halves[0]) + len(halves[1])),
        scratch_shapes=[pltpu.VMEM((3 * slots * rank, total), jnp.float32)],
        compiler_params=pltpu.CompilerParams(vmem_limit_bytes=LIMIT * MIB),
        name="add_delta",
    )(
        row_adapter, block_first, page_table, row_adapter.reshape(1, -1), shrunk, *ups, *nears, *bases, *raws,
    )
    return outs[: len(whole)], outs[len(whole) : len(whole) + len(halves[0])], outs[len(whole) + len(halves[0]) :]


def sum_kernel(count, *refs):
    wholes, parts, out = refs[: count[0]], refs[count[0] : -1], refs[-1]
    width = out.shape[1] // 2
    for h in range(2):
        columns = slice(h * width, (h + 1) * width)
        total = wholes[0][:, columns].astype(jnp.float32)
        for term in wholes[1:]:
            total = total + term[:, columns].astype(jnp.float32)
        for term in parts[: count[1]] if h == 0 else parts[count[1] :]:
            total = total + term[...].astype(jnp.float32)
        out[:, columns] = total.astype(out.dtype)


def add_up(wholes, firsts, seconds):
    return pl.pallas_call(
        functools.partial(sum_kernel, (len(wholes), len(firsts))),
        in_specs=[VMEM] * (len(wholes) + len(firsts) + len(seconds)),
        out_specs=VMEM,
        out_shape=jax.ShapeDtypeStruct(wholes[0].shape, jnp.bfloat16),
        compiler_params=pltpu.CompilerParams(vmem_limit_bytes=LIMIT * MIB),
        name="sum_rows",
    )(*wholes, *firsts, *seconds)


def plus_kernel(a, b, out):
    out[...] = a[...] + b[...]


def plus(a, b):
    return pl.pallas_call(
        plus_kernel,
        in_specs=[VMEM, VMEM],
        out_specs=VMEM,
        out_shape=jax.ShapeDtypeStruct(a.shape, a.dtype),
        compiler_params=pltpu.CompilerParams(vmem_limit_bytes=LIMIT * MIB),
        cost_estimate=pl.CostEstimate(flops=0, bytes_accessed=0, transcendentals=0),
        name="plus",
    )(a, b)


def local(
    n,
    tokens,
    gate_weight,
    up_weight,
    down_weight,
    adapter_down,
    adapter_up,
    row_adapter,
    block_first,
    page_table,
):
    blocks = [tokens] + [None] * (n - 1)
    far = [k for k in range(4, n) if k % 2 == 0]
    for k in far + [1, 2, 3]:
        blocks[k] = swap(tokens, "wide", n, k)
    gate_sent, gate_kept, up_first, *ups = fetch_gate(gate_weight, up_weight, adapter_up)
    last = far[-1]
    blocks[last], *ups = lax.optimization_barrier((blocks[last], *ups))
    for k in far:
        blocks[k ^ 1] = swap(blocks[k], "wide", n, 1)
    blocks[last], *blocks[1:4] = lax.optimization_barrier((blocks[last], *blocks[1:4]))
    up_sent, factors, *up_more = fetch_up(row_adapter, block_first, blocks[last], up_weight, adapter_down)
    sent, x = gate_up(blocks, gate_sent, [up_sent])
    got = swap(sent, "tensor", 2, 1)
    nears = [swap(piece, "wide", n, mask) for piece, (mask, _, _) in zip(ups, relays(n))]
    (kept,) = gate_up([x], gate_kept, [up_first, *up_more])
    mine = silu(kept, got)
    other = swap(mine, "tensor", 2, 1)
    shrunk = shrink(n, row_adapter, block_first, mine, other, factors)
    arrived = swap(shrunk, "wide", n, 1)
    shrunk, mine = lax.optimization_barrier((shrunk, mine))
    *sums, raw_x, raw_z = down(n, mine, other, down_weight)
    arrived, *rest = lax.optimization_barrier((arrived, *sums, raw_x, raw_z, *nears))
    bases, raws, nears = rest[:2], rest[2:4], rest[4:]
    shrunk = plus(shrunk, arrived)
    raws[0] = swap(raws[0], "wide", n, 1)
    bit = 2
    while bit < n:
        shrunk = plus(shrunk, swap(shrunk, "wide", n, bit))
        if bit == 2:
            shrunk, raws[1] = lax.optimization_barrier((shrunk, raws[1]))
            raws[1] = swap(raws[1], "wide", n, 2)
        bit *= 2
    parts = add_delta(n, row_adapter, block_first, page_table, shrunk, ups, nears, bases, raws)
    whole, halves = kept_blocks(n)
    arrived = {}
    for ks, xs in reversed(list(zip([whole] + halves, parts))):
        for k, block in reversed(list(zip(ks, xs))):
            arrived[k] = block if k == 0 else swap(block, "wide", n, k)
    last = [k for k in arrived if k > 2]
    arrived.update(zip(last, lax.optimization_barrier([arrived[k] for k in last])))
    arrived = [[arrived[k] for k in ks] for ks in [whole] + halves]
    return add_up(*arrived)


def solution(mesh):
    in_specs = (
        P(("parts", "wide"), "tensor"),
        P("tensor", "wide"),
        P("tensor", "wide"),
        P("wide", "tensor"),
        P("parts", None, "wide"),
        P(("parts", "wide"), None, "tensor"),
        P("parts"),
        P("parts"),
        P("parts"),
    )
    out_specs = P(("parts", "wide"), "tensor")
    body = functools.partial(local, mesh.shape["wide"])
    return jax.shard_map(body, mesh=mesh, in_specs=in_specs, out_specs=out_specs, check_vma=False)
```
